32 devices in a mesh: tm: 4 (over y, x), nrn: 8 (over z, core).
Axes of the slice: x: 2, y: 2, z: 4, core: 2. Of those that a mesh axis runs over, the one named last changes fastest.
Arguments:
- spikes: bfloat16 [8192, 32768], P('tm', 'nrn'), may hold values from -6 to 6
- read_in: bfloat16 [32768, 128], P('nrn'), may hold values from -0.03125 to 0.03125
- kernel: float32 [128, 8192], P(('tm', 'nrn')), may hold values from -0.0625 to 0.0625
- gain: float32 [128], replicated, may hold values from 0.1 to 1.9
- w_gate: bfloat16 [128, 512], replicated, may hold values from -0.5 to 0.5
- w_up: bfloat16 [128, 512], replicated, may hold values from -0.5 to 0.5
- w_down: bfloat16 [512, 128], replicated, may hold values from -0.25 to 0.25
Outputs:
- denoised: bfloat16 [8192, 128], P(('tm', 'nrn'))
The draws below stay inside these ranges and needn't reach their ends.
All inputs are finite; a program needn't handle non-finite values.
Results may differ from the reference program's by a relative error of at most 0.0045.
Values sent between devices are 32-bit elements; how exact they have to be, the bound alone decides.
A program may use at most 64 MiB of HBM per device.

```python
import jax
import jax.numpy as jnp
from jax import lax

NEURONS = 32768
LATENT = 128
HIDDEN_SIZE = 512
TIME = 8192


def block_scale(stream_key, extent, cuts, smallest, largest):
    def one(position, blocks):
        draws = jax.random.uniform(jax.random.fold_in(jax.random.fold_in(stream_key, 6), position), (blocks,), jnp.float32, smallest / len(cuts), largest / len(cuts))
        return jnp.repeat(jnp.exp(draws), extent[position] // blocks).reshape((-1,) + (1,) * (len(extent) - position - 1))

    level = one(*cuts[0])
    for cut in cuts[1:]:
        level = level * one(*cut)
    return level


def bell_draw(key, extent, deviation, most, pieces=(), held_as=jnp.bfloat16):
    result = deviation * jax.random.normal(key, extent, jnp.float32)
    if pieces:
        result = result * block_scale(key, extent, pieces, -0.22, 0.18)
    return jnp.clip(result, -most, most).astype(held_as)


def setup_inputs(seed: int = 0) -> dict:
    keys = jax.random.split(jax.random.key(seed), 8)
    return {
        "spikes": bell_draw(keys[0], (TIME, NEURONS), 1.0, 6.0, ((0, 4), (1, 8))),
        "read_in": bell_draw(keys[1], (NEURONS, LATENT), NEURONS ** -0.5, 0.03125, ((0, 8),)),
        "kernel": bell_draw(keys[2], (LATENT, TIME), TIME ** -0.5, 0.0625, ((0, 32),), jnp.float32),
        "gain": jnp.clip(1.0 + 0.18 * jax.random.normal(keys[3], (LATENT,), jnp.float32), 0.1, 1.9),
        "w_gate": bell_draw(keys[4], (LATENT, HIDDEN_SIZE), LATENT ** -0.5, 0.5),
        "w_up": bell_draw(keys[5], (LATENT, HIDDEN_SIZE), LATENT ** -0.5, 0.5),
        "w_down": bell_draw(keys[6], (HIDDEN_SIZE, LATENT), HIDDEN_SIZE ** -0.5, 0.25),
    }


def reference(spikes, read_in, kernel, gain, w_gate, w_up, w_down):
    latent = jnp.dot(spikes, read_in, preferred_element_type=jnp.float32)
    spectrum = jnp.fft.fft(latent.T, axis=-1) * jnp.fft.fft(kernel, axis=-1)
    conv = jnp.fft.ifft(spectrum, axis=-1).real.astype(jnp.float32).T
    mixed = latent + conv
    meansq = lax.optimization_barrier(jnp.mean(mixed * mixed, axis=-1, keepdims=True))
    normed = (mixed * jax.lax.rsqrt(meansq + 1e-05) * gain).astype(jnp.bfloat16)
    gate = jnp.dot(normed, w_gate, preferred_element_type=jnp.float32)
    upper = jnp.dot(normed, w_up, preferred_element_type=jnp.float32)
    act = (jax.nn.silu(gate) * upper).astype(jnp.bfloat16)
    return (mixed + jnp.dot(act, w_down, preferred_element_type=jnp.float32)).astype(jnp.bfloat16)
```

```python
import math

import jax
import jax.numpy as jnp
import ml_dtypes
import numpy as np
from jax import lax
from jax.experimental import pallas as pl
from jax.experimental.pallas import tpu as pltpu
from jax.sharding import PartitionSpec as P

MESH = pl.DeviceIdType.MESH
TILE_BINS = 1
TILES = 8
AHEAD = 3
LAG = 5

precise = lax.Precision.HIGHEST


def dft_table(order):
    index = jnp.arange(order, dtype=jnp.int32)
    phase = index[:, None] * index[None, :] % order
    angles = phase.astype(jnp.float32) * (2.0 * math.pi / order)
    return (jnp.cos(angles), jnp.sin(angles))


def twiddle_table(outer, inner):
    outer_index = jnp.arange(outer, dtype=jnp.int32)
    inner_index = jnp.arange(inner, dtype=jnp.int32)
    phase = outer_index[:, None] * inner_index[None, :] % (outer * inner)
    angles = phase.astype(jnp.float32) * (2.0 * math.pi / (outer * inner))
    return (jnp.cos(angles), jnp.sin(angles))


def forward_dft(signal, tables):
    cos_outer, sin_outer, cos_twist, sin_twist, cos_inner, sin_inner = tables
    real_part = jnp.einsum("ar,crs->cas", cos_outer, signal, precision=precise)
    imag_part = -jnp.einsum("ar,crs->cas", sin_outer, signal, precision=precise)
    twist_real = real_part * cos_twist + imag_part * sin_twist
    twist_imag = imag_part * cos_twist - real_part * sin_twist
    spec_real = jnp.einsum("cas,sb->cab", twist_real, cos_inner, precision=precise) + jnp.einsum(
        "cas,sb->cab", twist_imag, sin_inner, precision=precise
    )
    spec_imag = jnp.einsum("cas,sb->cab", twist_imag, cos_inner, precision=precise) - jnp.einsum(
        "cas,sb->cab", twist_real, sin_inner, precision=precise
    )
    return (spec_real, spec_imag)


def inverse_dft(spec_real, spec_imag, tables):
    cos_outer, sin_outer, cos_twist, sin_twist, cos_inner, sin_inner = tables
    back_real = jnp.einsum("cab,bs->cas", spec_real, cos_inner, precision=precise) - jnp.einsum(
        "cab,bs->cas", spec_imag, sin_inner, precision=precise
    )
    back_imag = jnp.einsum("cab,bs->cas", spec_real, sin_inner, precision=precise) + jnp.einsum(
        "cab,bs->cas", spec_imag, cos_inner, precision=precise
    )
    turn_real = back_real * cos_twist - back_imag * sin_twist
    turn_imag = back_real * sin_twist + back_imag * cos_twist
    result = jnp.einsum("ra,cas->crs", cos_outer, turn_real, precision=precise) - jnp.einsum(
        "ra,cas->crs", sin_outer, turn_imag, precision=precise
    )
    return result / (cos_outer.shape[0] * cos_inner.shape[0])


def per_device(spikes, read_in, kernel, gain, w_gate, w_up, w_down):
    time_groups = lax.axis_size("tm")
    neuron_groups = lax.axis_size("nrn")
    devices = time_groups * neuron_groups
    tok_rows = spikes.shape[0] // neuron_groups
    latent_width = read_in.shape[1]
    channels_dev = latent_width // devices
    session = tok_rows * devices
    latent = lax.psum_scatter(
        jnp.dot(spikes, read_in, preferred_element_type=jnp.float32),
        "nrn",
        scatter_dimension=0,
        tiled=True,
    )
    flipped = latent.T
    series = lax.all_to_all(flipped, ("tm", "nrn"), split_axis=0, concat_axis=1, tiled=True)
    cos_outer, sin_outer = dft_table(devices)
    cos_inner, sin_inner = dft_table(tok_rows)
    cos_twist, sin_twist = twiddle_table(devices, tok_rows)
    tables = (cos_outer, sin_outer, cos_twist, sin_twist, cos_inner, sin_inner)
    data_real, data_imag = forward_dft(series.reshape(channels_dev, devices, tok_rows), tables)
    kern_real, kern_imag = forward_dft(kernel.reshape(channels_dev, devices, tok_rows), tables)
    prod_real = data_real * kern_real - data_imag * kern_imag
    prod_imag = data_real * kern_imag + data_imag * kern_real
    conv = inverse_dft(prod_real, prod_imag, tables).reshape(channels_dev, session)
    mixed = series + conv
    stacked = lax.all_to_all(mixed, ("tm", "nrn"), split_axis=1, concat_axis=0, tiled=True)
    residual = stacked.T
    meansq = jnp.mean(residual * residual, axis=-1, keepdims=True)
    normed = (residual * lax.rsqrt(meansq + 1e-05) * gain).astype(jnp.bfloat16)
    gate = jnp.dot(normed, w_gate, preferred_element_type=jnp.float32)
    upper = jnp.dot(normed, w_up, preferred_element_type=jnp.float32)
    act = (jax.nn.silu(gate) * upper).astype(jnp.bfloat16)
    return (residual + jnp.dot(act, w_down, preferred_element_type=jnp.float32)).astype(
        jnp.bfloat16
    )


def split(value):
    high = value.astype(jnp.bfloat16)
    low = (value - high.astype(jnp.float32)).astype(jnp.bfloat16)
    return high, low


def session_tables():
    outer, inner = 32, 256
    angle = lambda rows, columns, order: (
        2.0 * np.pi / order * (np.outer(np.arange(rows), np.arange(columns)) % order)
    )

    def parts(table):
        table = table.astype(np.float32)
        high = table.astype(ml_dtypes.bfloat16)
        low = (table - high.astype(np.float32)).astype(ml_dtypes.bfloat16)
        return high, low

    around = angle(outer, outer, outer)
    high, low = parts(np.concatenate([np.cos(around), -np.sin(around)], 0))
    first = np.concatenate([high, low, high], 1)
    high, low = parts(np.concatenate([np.cos(around), -np.sin(around)], 1))
    last = np.concatenate([high, low, high], 1)
    within = angle(inner, inner, inner)
    cosine, sine = np.cos(within), np.sin(within)
    mid_high, mid_low = parts(np.block([[cosine, -sine], [sine, cosine]]))
    turn = angle(outer, inner, outer * inner)
    twist = np.stack([np.cos(turn), np.sin(turn)]).astype(np.float32)
    return first, last, np.stack([mid_high, mid_low]), twist


def fused_kernel(
    spikes, read_in, kernel, gain, w_gate, w_up, w_down, first, last, middle, twist,
    out,
    spk_v, rd_v, ker_v, wg_v, wu_v, wd_v, first_v, last_v, mid_v, twist_v,
    own, sib, acc, from_end, fwd, from_inner, to_end, from_mid, xsend, xall, kall, ysend, yall, spec,
    spk_sem, tab_sem, sib_s, sib_r, end_s, end_r, inn_s, inn_r, fin_s, fin_r, x_s, x_r, y_s, y_r,
):
    tm, nrn = lax.axis_index("tm"), lax.axis_index("nrn")
    me = tm * 8 + nrn
    z, core = nrn // 2, nrn % 2
    is_end = (z == 0) | (z == 3)
    is_inner = (z == 1) | (z == 2)
    rows = TILE_BINS * 256

    def spike_copy(k):
        return pltpu.make_async_copy(
            spikes.at[pl.ds(pl.multiple_of(k * rows, rows), rows)], spk_v.at[k], spk_sem.at[k]
        )

    loads = [
        pltpu.make_async_copy(source, target, tab_sem.at[i])
        for i, (source, target) in enumerate(
            [
                (read_in, rd_v), (kernel, ker_v), (first, first_v), (twist, twist_v),
                (middle, mid_v), (last, last_v), (w_gate, wg_v), (w_up, wu_v), (w_down, wd_v),
            ]
        )
    ]
    loads[0].start()
    for k in range(AHEAD):
        spike_copy(k).start()
    for load in loads[1:]:
        load.start()

    barrier = pltpu.get_barrier_semaphore()

    def greet(d, carry):
        other = (me + d) % 32
        pl.semaphore_signal(barrier, inc=1, device_id=(other // 8, other % 8), device_id_type=MESH)
        return carry

    lax.fori_loop(1, 32, greet, 0)
    loads[0].wait()
    pl.semaphore_wait(barrier, 31)

    def remote(source, target, send, recv, where):
        return pltpu.make_async_remote_copy(
            src_ref=source, dst_ref=target, send_sem=send, recv_sem=recv,
            device_id=where, device_id_type=MESH,
        )

    def at_z(place):
        return (tm, place * 2 + core)

    def sib_copy(k):
        return remote(own.at[k, 1 - core], sib.at[k], sib_s.at[k], sib_r.at[k], (tm, z * 2 + 1 - core))

    end_inner = jnp.where(z == 0, 1, 2)
    end_first = jnp.where(z == 0, 1, 0)
    near_end = jnp.where(z == 1, 0, 3)
    fwd_first = jnp.where(z == 1, 2, 0)
    own_slot = z % 2

    def end_copy(k):
        return remote(
            acc.at[k, pl.ds(end_first, 3)], from_end.at[k, pl.ds(end_first, 3)],
            end_s.at[k], end_r.at[k], at_z(end_inner),
        )

    def inner_copy(k):
        return remote(fwd.at[k], from_inner.at[k], inn_s.at[k], inn_r.at[k], at_z(3 - z))

    def final_copy(k):
        return remote(to_end.at[k], from_mid.at[k], fin_s.at[k], fin_r.at[k], at_z(near_end))

    def x_copy(k, d):
        other = (tm + d) % 4
        return remote(
            xsend.at[k, other], xall.at[pl.ds(tm * 8 + k * TILE_BINS, TILE_BINS)],
            x_s.at[k, d], x_r.at[k, d], (other, nrn),
        )

    def project(k):
        spike_copy(k).wait()
        sums = jnp.dot(spk_v[k], rd_v[...], preferred_element_type=jnp.float32)
        for b in range(TILE_BINS):
            low = sums[b * 256 : b * 256 + 128].T
            high = sums[b * 256 + 128 : b * 256 + 256].T
            for g in range(32):
                piece = jnp.concatenate([low[4 * g : 4 * g + 4], high[4 * g : 4 * g + 4]], 0)
                own[k, g % 2, (g % 8) // 2, g // 8, b] = piece
        sib_copy(k).start()

    def pair(k):
        sib_copy(k).wait_recv()
        acc[k] = own[k, core] + sib[k]

        @pl.when(is_end)
        def _():
            end_copy(k).start()

    def forward_sum(k):
        @pl.when(is_inner)
        def _():
            end_copy(k).wait_recv()
            fwd[k] = acc[k, pl.ds(fwd_first, 2)] + from_end[k, pl.ds(fwd_first, 2)]
            inner_copy(k).start()

    def finish_sum(k):
        @pl.when(is_inner)
        def _():
            inner_copy(k).wait_recv()
            to_end[k] = acc[k, near_end] + from_inner[k, 1 - own_slot]
            final_copy(k).start()
            xsend[k] = acc[k, z] + from_end[k, z] + from_inner[k, own_slot]

        @pl.when(is_end)
        def _():
            final_copy(k).wait_recv()
            xsend[k] = acc[k, z] + from_mid[k]

        for d in (3, 1, 2):
            x_copy(k, d).start()
        xall[pl.ds(tm * 8 + k * TILE_BINS, TILE_BINS)] = xsend[k, tm]

    def tile_step(k, carry):
        @pl.when(k + AHEAD < TILES)
        def _():
            spike_copy(k + AHEAD).start()

        project(k)

        @pl.when(k >= 1)
        def _():
            pair(k - 1)

        @pl.when(k >= LAG)
        def _():
            forward_sum(k - LAG)

        return carry

    lax.fori_loop(0, TILES, tile_step, 0)
    pair(TILES - 1)

    for load in loads[1:]:
        load.wait()
    for r in range(32):
        for half in range(2):
            kall[r, half * 4 : half * 4 + 4, :] = ker_v[:, r * 256 + half * 128 : r * 256 + half * 128 + 128]

    cos_turn = jnp.concatenate([twist_v[0]] * 4, 1)
    sin_turn = jnp.concatenate([twist_v[1]] * 4, 1)

    def stacked(value):
        high, low = split(value)
        return jnp.concatenate([high, high, low], 0)

    def to_rows(value):
        return jnp.concatenate([value[:, 256 * j : 256 * j + 256] for j in range(4)], 0)

    def to_lanes(value):
        return jnp.concatenate([value[32 * j : 32 * j + 32] for j in range(4)], 1)

    def inner_dft(real, imag):
        high, low = split(jnp.concatenate([real, imag], 1))
        result = jnp.dot(high, mid_v[0], preferred_element_type=jnp.float32)
        result += jnp.dot(high, mid_v[1], preferred_element_type=jnp.float32)
        result += jnp.dot(low, mid_v[0], preferred_element_type=jnp.float32)
        return result[:, :256], result[:, 256:]

    def gather_lanes(ref):
        return jnp.concatenate([ref[:, half * 4 + j, :] for j in range(4) for half in range(2)], 1)

    def forward_dft(signal):
        both = jnp.dot(first_v[...], stacked(signal), preferred_element_type=jnp.float32)
        real, imag = both[:32], both[32:]
        turned_real = real * cos_turn + imag * sin_turn
        turned_imag = imag * cos_turn - real * sin_turn
        return inner_dft(to_rows(turned_real), to_rows(turned_imag))

    kern_real, kern_imag = forward_dft(gather_lanes(kall))
    spec[0] = kern_real * (1.0 / 8192)
    spec[1] = kern_imag * (1.0 / 8192)

    def late_forward(k, carry):
        forward_sum(k)

        @pl.when(k > TILES - LAG)
        def _():
            finish_sum(k - 1)

        return carry

    def early_finish(k, carry):
        finish_sum(k)
        return carry

    lax.fori_loop(TILES - LAG, TILES - LAG + 1, late_forward, 0)
    lax.fori_loop(0, TILES - LAG, early_finish, 0)
    lax.fori_loop(TILES - LAG + 1, TILES, late_forward, 0)
    finish_sum(TILES - 1)

    def x_arrived(k, carry):
        for d in (1, 2, 3):
            x_copy(k, d).wait_recv()
        return carry

    lax.fori_loop(0, TILES, x_arrived, 0)

    series = gather_lanes(xall)
    data_real, data_imag = forward_dft(series)
    prod_real = data_real * spec[0] - data_imag * spec[1]
    prod_imag = data_real * spec[1] + data_imag * spec[0]
    back_real, back_neg = inner_dft(prod_real, -prod_imag)
    back_real, back_neg = to_lanes(back_real), to_lanes(back_neg)
    turned = jnp.concatenate(
        [back_real * cos_turn + back_neg * sin_turn, back_real * sin_turn - back_neg * cos_turn], 0
    )
    mixed = series + jnp.dot(last_v[...], stacked(turned), preferred_element_type=jnp.float32)
    for m in range(8):
        ysend[:, m, :] = mixed[:, 128 * m : 128 * m + 128]

    def y_copy(d):
        other = (me + d) % 32
        return remote(ysend.at[other], yall.at[me], y_s.at[d], y_r.at[d], (other // 8, other % 8))

    def y_start(d, carry):
        y_copy(d).start()
        return carry

    lax.fori_loop(1, 32, y_start, 0)
    yall[me] = ysend[me]

    def drain(k, carry):
        sib_copy(k).wait_send()

        @pl.when(is_end)
        def _():
            end_copy(k).wait_send()

        @pl.when(is_inner)
        def _():
            inner_copy(k).wait_send()
            final_copy(k).wait_send()

        for d in (1, 2, 3):
            x_copy(k, d).wait_send()
        return carry

    lax.fori_loop(0, TILES, drain, 0)

    def y_wait(d, carry):
        y_copy(d).wait()
        return carry

    lax.fori_loop(1, 32, y_wait, 0)

    flat = yall.reshape(256, 128)
    residual = jnp.concatenate([flat[pl.ds(half, 128, stride=2), :].T for half in range(2)], 0)
    meansq = jnp.mean(residual * residual, axis=-1, keepdims=True)
    normed = (residual * lax.rsqrt(meansq + 1e-05) * gain[...]).astype(jnp.bfloat16)
    gate = jnp.dot(normed, wg_v[...], preferred_element_type=jnp.float32)
    upper = jnp.dot(normed, wu_v[...], preferred_element_type=jnp.float32)
    act = (gate / (1.0 + jnp.exp(-gate)) * upper).astype(jnp.bfloat16)
    out[...] = (residual + jnp.dot(act, wd_v[...], preferred_element_type=jnp.float32)).astype(jnp.bfloat16)


def fused(spikes, read_in, kernel, gain, w_gate, w_up, w_down):
    first, last, middle, twist = session_tables()
    f32, bf16 = jnp.float32, jnp.bfloat16
    tile = (TILE_BINS, 8, 128)
    rows = TILE_BINS * 256
    dma = pltpu.SemaphoreType.DMA
    anywhere = pl.BlockSpec(memory_space=pl.ANY)
    vmem = pl.BlockSpec(memory_space=pltpu.VMEM)
    return pl.pallas_call(
        fused_kernel,
        out_shape=jax.ShapeDtypeStruct((256, 128), bf16),
        in_specs=[anywhere] * 3 + [vmem] + [anywhere] * 7,
        out_specs=vmem,
        scratch_shapes=[
            pltpu.VMEM((TILES, rows, 4096), bf16),
            pltpu.VMEM((4096, 128), bf16),
            pltpu.VMEM((4, 8192), f32),
            pltpu.VMEM((128, 512), bf16),
            pltpu.VMEM((128, 512), bf16),
            pltpu.VMEM((512, 128), bf16),
            pltpu.VMEM(first.shape, bf16),
            pltpu.VMEM(last.shape, bf16),
            pltpu.VMEM(middle.shape, bf16),
            pltpu.VMEM(twist.shape, f32),
            pltpu.VMEM((TILES, 2, 4, 4) + tile, f32),
            pltpu.VMEM((TILES, 4, 4) + tile, f32),
            pltpu.VMEM((TILES, 4, 4) + tile, f32),
            pltpu.VMEM((TILES, 4, 4) + tile, f32),
            pltpu.VMEM((TILES, 2, 4) + tile, f32),
            pltpu.VMEM((TILES, 2, 4) + tile, f32),
            pltpu.VMEM((TILES, 4) + tile, f32),
            pltpu.VMEM((TILES, 4) + tile, f32),
            pltpu.VMEM((TILES, 4) + tile, f32),
            pltpu.VMEM((32, 8, 128), f32),
            pltpu.VMEM((32, 8, 128), f32),
            pltpu.VMEM((32, 8, 128), f32),
            pltpu.VMEM((32, 8, 128), f32),
            pltpu.VMEM((2, 128, 256), f32),
            dma((TILES,)), dma((9,)),
            dma((TILES,)), dma((TILES,)), dma((TILES,)), dma((TILES,)),
            dma((TILES,)), dma((TILES,)), dma((TILES,)), dma((TILES,)),
            dma((TILES, 4)), dma((TILES, 4)), dma((32,)), dma((32,)),
        ],
        compiler_params=pltpu.CompilerParams(
            collective_id=0, has_side_effects=True, vmem_limit_bytes=56 * 1024 * 1024
        ),
    )(
        spikes, read_in, kernel, gain.reshape(1, 128), w_gate, w_up, w_down,
        jnp.asarray(first), jnp.asarray(last), jnp.asarray(middle), jnp.asarray(twist),
    )


def solution(mesh):
    placed = (P("tm", "nrn"), P("nrn", None), P(("tm", "nrn"), None), P(), P(), P(), P())
    small = mesh.shape["tm"] == 4 and mesh.shape["nrn"] == 8
    return jax.shard_map(
        fused if small else per_device,
        mesh=mesh, in_specs=placed, out_specs=P(("tm", "nrn"), None), check_vma=False,
    )
```

```python
import math

import jax
import jax.numpy as jnp
import ml_dtypes
import numpy as np
from jax import lax
from jax.experimental import pallas as pl
from jax.experimental.pallas import tpu as pltpu
from jax.sharding import PartitionSpec as P

MESH = pl.DeviceIdType.MESH
TILE_BINS = 1
TILES = 8

precise = lax.Precision.HIGHEST


def dft_table(order):
    index = jnp.arange(order, dtype=jnp.int32)
    phase = index[:, None] * index[None, :] % order
    angles = phase.astype(jnp.float32) * (2.0 * math.pi / order)
    return (jnp.cos(angles), jnp.sin(angles))


def twiddle_table(outer, inner):
    outer_index = jnp.arange(outer, dtype=jnp.int32)
    inner_index = jnp.arange(inner, dtype=jnp.int32)
    phase = outer_index[:, None] * inner_index[None, :] % (outer * inner)
    angles = phase.astype(jnp.float32) * (2.0 * math.pi / (outer * inner))
    return (jnp.cos(angles), jnp.sin(angles))


def forward_dft(signal, tables):
    cos_outer, sin_outer, cos_twist, sin_twist, cos_inner, sin_inner = tables
    real_part = jnp.einsum("ar,crs->cas", cos_outer, signal, precision=precise)
    imag_part = -jnp.einsum("ar,crs->cas", sin_outer, signal, precision=precise)
    twist_real = real_part * cos_twist + imag_part * sin_twist
    twist_imag = imag_part * cos_twist - real_part * sin_twist
    spec_real = jnp.einsum("cas,sb->cab", twist_real, cos_inner, precision=precise) + jnp.einsum(
        "cas,sb->cab", twist_imag, sin_inner, precision=precise
    )
    spec_imag = jnp.einsum("cas,sb->cab", twist_imag, cos_inner, precision=precise) - jnp.einsum(
        "cas,sb->cab", twist_real, sin_inner, precision=precise
    )
    return (spec_real, spec_imag)


def inverse_dft(spec_real, spec_imag, tables):
    cos_outer, sin_outer, cos_twist, sin_twist, cos_inner, sin_inner = tables
    back_real = jnp.einsum("cab,bs->cas", spec_real, cos_inner, precision=precise) - jnp.einsum(
        "cab,bs->cas", spec_imag, sin_inner, precision=precise
    )
    back_imag = jnp.einsum("cab,bs->cas", spec_real, sin_inner, precision=precise) + jnp.einsum(
        "cab,bs->cas", spec_imag, cos_inner, precision=precise
    )
    turn_real = back_real * cos_twist - back_imag * sin_twist
    turn_imag = back_real * sin_twist + back_imag * cos_twist
    result = jnp.einsum("ra,cas->crs", cos_outer, turn_real, precision=precise) - jnp.einsum(
        "ra,cas->crs", sin_outer, turn_imag, precision=precise
    )
    return result / (cos_outer.shape[0] * cos_inner.shape[0])


def per_device(spikes, read_in, kernel, gain, w_gate, w_up, w_down):
    time_groups = lax.axis_size("tm")
    neuron_groups = lax.axis_size("nrn")
    devices = time_groups * neuron_groups
    tok_rows = spikes.shape[0] // neuron_groups
    latent_width = read_in.shape[1]
    channels_dev = latent_width // devices
    session = tok_rows * devices
    latent = lax.psum_scatter(
        jnp.dot(spikes, read_in, preferred_element_type=jnp.float32),
        "nrn",
        scatter_dimension=0,
        tiled=True,
    )
    flipped = latent.T
    series = lax.all_to_all(flipped, ("tm", "nrn"), split_axis=0, concat_axis=1, tiled=True)
    cos_outer, sin_outer = dft_table(devices)
    cos_inner, sin_inner = dft_table(tok_rows)
    cos_twist, sin_twist = twiddle_table(devices, tok_rows)
    tables = (cos_outer, sin_outer, cos_twist, sin_twist, cos_inner, sin_inner)
    data_real, data_imag = forward_dft(series.reshape(channels_dev, devices, tok_rows), tables)
    kern_real, kern_imag = forward_dft(kernel.reshape(channels_dev, devices, tok_rows), tables)
    prod_real = data_real * kern_real - data_imag * kern_imag
    prod_imag = data_real * kern_imag + data_imag * kern_real
    conv = inverse_dft(prod_real, prod_imag, tables).reshape(channels_dev, session)
    mixed = series + conv
    stacked = lax.all_to_all(mixed, ("tm", "nrn"), split_axis=1, concat_axis=0, tiled=True)
    residual = stacked.T
    meansq = jnp.mean(residual * residual, axis=-1, keepdims=True)
    normed = (residual * lax.rsqrt(meansq + 1e-05) * gain).astype(jnp.bfloat16)
    gate = jnp.dot(normed, w_gate, preferred_element_type=jnp.float32)
    upper = jnp.dot(normed, w_up, preferred_element_type=jnp.float32)
    act = (jax.nn.silu(gate) * upper).astype(jnp.bfloat16)
    return (residual + jnp.dot(act, w_down, preferred_element_type=jnp.float32)).astype(
        jnp.bfloat16
    )


def split(value):
    high = value.astype(jnp.bfloat16)
    low = (value - high.astype(jnp.float32)).astype(jnp.bfloat16)
    return high, low


def session_tables():
    outer, inner = 32, 256
    angle = lambda rows, columns, order: (
        2.0 * np.pi / order * (np.outer(np.arange(rows), np.arange(columns)) % order)
    )

    def parts(table):
        table = table.astype(np.float32)
        high = table.astype(ml_dtypes.bfloat16)
        low = (table - high.astype(np.float32)).astype(ml_dtypes.bfloat16)
        return high, low

    around = angle(outer, outer, outer)
    high, low = parts(np.concatenate([np.cos(around), -np.sin(around)], 0))
    first = np.concatenate([high, low, high], 1)
    high, low = parts(np.concatenate([np.cos(around), -np.sin(around)], 1))
    last = np.concatenate([high, low, high], 1)
    within = angle(inner, inner, inner)
    cosine, sine = np.cos(within), np.sin(within)
    mid_high, mid_low = parts(np.block([[cosine, -sine], [sine, cosine]]))
    turn = angle(outer, inner, outer * inner)
    twist = np.stack([np.cos(turn), np.sin(turn)]).astype(np.float32)
    return first, last, np.stack([mid_high, mid_low]), twist


def fused_kernel(
    spikes, read_in, kernel, gain, w_gate, w_up, w_down, first, last, middle, twist,
    out,
    spk_v, rd_v, ker_v, wg_v, wu_v, wd_v, first_v, last_v, mid_v, twist_v,
    own, sib, acc, from_end, fwd, from_inner, to_end, from_mid, xsend, xall, kall, ysend, yall, spec,
    spk_sem, tab_sem, sib_s, sib_r, end_s, end_r, inn_s, inn_r, fin_s, fin_r, x_s, x_r, y_s, y_r,
):
    tm, nrn = lax.axis_index("tm"), lax.axis_index("nrn")
    me = tm * 8 + nrn
    z, core = lax.div(nrn, 2), lax.rem(nrn, 2)
    is_end = (z == 0) | (z == 3)
    is_inner = (z == 1) | (z == 2)
    rows = TILE_BINS * 256

    def spike_copy(k):
        where = pl.ds(k * rows, rows)
        return pltpu.make_async_copy(spikes.at[where], spk_v.at[where], spk_sem.at[k])

    loads = [
        pltpu.make_async_copy(source, target, tab_sem.at[i])
        for i, (source, target) in enumerate(
            [
                (read_in, rd_v), (kernel, ker_v), (first, first_v), (twist, twist_v),
                (middle, mid_v), (last, last_v), (w_gate, wg_v), (w_up, wu_v), (w_down, wd_v),
            ]
        )
    ]
    loads[0].start()
    for k in range(4):
        spike_copy(k).start()

    barrier = pltpu.get_barrier_semaphore()

    def after(d):
        other = lax.rem(me + d, 32)
        return (lax.div(other, 8), lax.rem(other, 8))

    def greet(d, carry):
        pl.semaphore_signal(barrier, inc=1, device_id=after(d), device_id_type=MESH)
        return carry

    lax.fori_loop(1, 32, greet, 0)
    loads[0].wait()
    pl.semaphore_wait(barrier, 31)

    def remote(source, target, send, recv, where):
        return pltpu.make_async_remote_copy(
            src_ref=source, dst_ref=target, send_sem=send, recv_sem=recv,
            device_id=where, device_id_type=MESH,
        )

    def at_z(place):
        return (tm, place * 2 + core)

    def sib_copy(k):
        return remote(own.at[k, 1 - core], sib.at[k], sib_s.at[k], sib_r.at[k], (tm, z * 2 + 1 - core))

    end_inner = jnp.where(z == 0, 1, 2)
    end_first = jnp.where(z == 0, 1, 0)
    near_end = jnp.where(z == 1, 0, 3)
    fwd_first = jnp.where(z == 1, 2, 0)
    own_slot = lax.rem(z, 2)

    def end_copy(k):
        return remote(
            acc.at[k, pl.ds(end_first, 3)], from_end.at[k, pl.ds(end_first, 3)],
            end_s.at[k], end_r.at[k], at_z(end_inner),
        )

    def inner_copy(k):
        return remote(fwd.at[k], from_inner.at[k], inn_s.at[k], inn_r.at[k], at_z(3 - z))

    def final_copy(k):
        return remote(to_end.at[k], from_mid.at[k], fin_s.at[k], fin_r.at[k], at_z(near_end))

    def x_copy(k, d):
        other = lax.rem(tm + d, 4)
        return remote(
            xsend.at[k, other], xall.at[pl.ds(tm * 8 + k * TILE_BINS, TILE_BINS)],
            x_s.at[k, d], x_r.at[k, d], (other, nrn),
        )

    def project(start, count):
        for k in range(start, start + count):
            spike_copy(k).wait()
        block = spk_v[start * rows : (start + count) * rows]
        sums = jnp.dot(block, rd_v[...], preferred_element_type=jnp.float32)
        for i in range(count):
            for b in range(TILE_BINS):
                at = i * rows + b * 256
                low, high = sums[at : at + 128].T, sums[at + 128 : at + 256].T
                for g in range(32):
                    piece = jnp.concatenate([low[4 * g : 4 * g + 4], high[4 * g : 4 * g + 4]], 0)
                    own[start + i, g % 2, (g % 8) // 2, g // 8, b] = piece
            sib_copy(start + i).start()

    def pair(k):
        sib_copy(k).wait_recv()
        acc[k] = own[k, core] + sib[k]

        @pl.when(is_end)
        def _():
            end_copy(k).start()

    def forward_sum(k):
        @pl.when(is_inner)
        def _():
            end_copy(k).wait_recv()
            fwd[k] = acc[k, pl.ds(fwd_first, 2)] + from_end[k, pl.ds(fwd_first, 2)]
            inner_copy(k).start()

    def finish_sum(k):
        @pl.when(is_inner)
        def _():
            inner_copy(k).wait_recv()
            to_end[k] = acc[k, near_end] + from_inner[k, 1 - own_slot]
            final_copy(k).start()
            xsend[k] = acc[k, z] + from_end[k, z] + from_inner[k, own_slot]

        @pl.when(is_end)
        def _():
            final_copy(k).wait_recv()
            xsend[k] = acc[k, z] + from_mid[k]

        for d in (3, 1, 2):
            x_copy(k, d).start()
        xall[pl.ds(tm * 8 + k * TILE_BINS, TILE_BINS)] = xsend[k, tm]

    def each(step, start, stop):
        def body(k, carry):
            step(k)
            return carry

        lax.fori_loop(start, stop, body, 0)

    project(0, 1)
    for k in range(4, TILES):
        spike_copy(k).start()
    for load in loads[1:]:
        load.start()
    project(1, 1)
    pair(0)
    project(2, 2)
    pair(1)
    project(4, 2)
    each(pair, 2, 4)
    each(forward_sum, 0, 2)
    project(6, 2)
    each(pair, 4, 6)
    forward_sum(2)
    each(pair, 6, 8)

    for load in loads[1:]:
        load.wait()
    for r in range(32):
        for half in range(2):
            kall[r, half * 4 : half * 4 + 4, :] = ker_v[:, r * 256 + half * 128 : r * 256 + half * 128 + 128]

    cos_turn = jnp.concatenate([twist_v[0]] * 4, 1)
    sin_turn = jnp.concatenate([twist_v[1]] * 4, 1)

    def stacked(value):
        high, low = split(value)
        return jnp.concatenate([high, high, low], 0)

    def to_rows(value):
        return jnp.concatenate([value[:, 256 * j : 256 * j + 256] for j in range(4)], 0)

    def to_lanes(value):
        return jnp.concatenate([value[32 * j : 32 * j + 32] for j in range(4)], 1)

    def inner_dft(real, imag):
        high, low = split(jnp.concatenate([real, imag], 1))
        both = jnp.concatenate([high, low], 0)
        result = jnp.dot(both, mid_v[0], preferred_element_type=jnp.float32)
        result = result[:128] + result[128:]
        result += jnp.dot(high, mid_v[1], preferred_element_type=jnp.float32)
        return result[:, :256], result[:, 256:]

    def gather_lanes(ref):
        return jnp.concatenate([ref[:, half * 4 + j, :] for j in range(4) for half in range(2)], 1)

    def outer_dft(signal):
        both = jnp.dot(first_v[...], stacked(signal), preferred_element_type=jnp.float32)
        real, imag = both[:32], both[32:]
        turned_real = real * cos_turn + imag * sin_turn
        turned_imag = imag * cos_turn - real * sin_turn
        return to_rows(turned_real), to_rows(turned_imag)

    spec[0], spec[1] = outer_dft(gather_lanes(kall))

    def forward_then_finish(k):
        forward_sum(k)
        finish_sum(k - 2)

    forward_sum(3)
    each(finish_sum, 0, 2)
    each(forward_then_finish, 4, 6)
    kern_real, kern_imag = inner_dft(spec[0], spec[1])
    spec[0] = kern_real * (1.0 / 8192)
    spec[1] = kern_imag * (1.0 / 8192)
    each(forward_then_finish, 6, 8)
    each(finish_sum, 6, 8)

    def x_arrived(k, carry):
        for d in (1, 2, 3):
            x_copy(k, d).wait_recv()
        return carry

    lax.fori_loop(0, TILES, x_arrived, 0)

    series = gather_lanes(xall)
    data_real, data_imag = inner_dft(*outer_dft(series))
    prod_real = data_real * spec[0] - data_imag * spec[1]
    prod_imag = data_real * spec[1] + data_imag * spec[0]
    back_real, back_neg = inner_dft(prod_real, -prod_imag)
    back_real, back_neg = to_lanes(back_real), to_lanes(back_neg)
    turned = jnp.concatenate(
        [back_real * cos_turn + back_neg * sin_turn, back_real * sin_turn - back_neg * cos_turn], 0
    )
    mixed = series + jnp.dot(last_v[...], stacked(turned), preferred_element_type=jnp.float32)
    for m in range(8):
        ysend[:, m, :] = mixed[:, 128 * m : 128 * m + 128]

    def y_copy(d):
        other = lax.rem(me + d, 32)
        return remote(ysend.at[other], yall.at[me], y_s.at[d], y_r.at[d], after(d))

    for d in range(1, 32):
        y_copy(d).start()
    yall[me] = ysend[me]

    def drain(k, carry):
        sib_copy(k).wait_send()

        @pl.when(is_end)
        def _():
            end_copy(k).wait_send()

        @pl.when(is_inner)
        def _():
            inner_copy(k).wait_send()
            final_copy(k).wait_send()

        for d in (1, 2, 3):
            x_copy(k, d).wait_send()
        return carry

    lax.fori_loop(0, TILES, drain, 0)

    def y_wait(d, carry):
        y_copy(d).wait()
        return carry

    lax.fori_loop(1, 32, y_wait, 0)

    flat = yall.reshape(256, 128)
    residual = jnp.concatenate([flat[pl.ds(half, 128, stride=2), :].T for half in range(2)], 0)
    meansq = jnp.mean(residual * residual, axis=-1, keepdims=True)
    normed = (residual * lax.rsqrt(meansq + 1e-05) * gain[...]).astype(jnp.bfloat16)
    gate = jnp.dot(normed, wg_v[...], preferred_element_type=jnp.float32)
    upper = jnp.dot(normed, wu_v[...], preferred_element_type=jnp.float32)
    act = (gate / (1.0 + jnp.exp(-gate)) * upper).astype(jnp.bfloat16)
    out[...] = residual + jnp.dot(act, wd_v[...], preferred_element_type=jnp.float32)


def fused(spikes, read_in, kernel, gain, w_gate, w_up, w_down):
    first, last, middle, twist = session_tables()
    f32, bf16 = jnp.float32, jnp.bfloat16
    tile = (TILE_BINS, 8, 128)
    rows = TILE_BINS * 256
    dma = pltpu.SemaphoreType.DMA
    anywhere = pl.BlockSpec(memory_space=pl.ANY)
    vmem = pl.BlockSpec(memory_space=pltpu.VMEM)
    return pl.pallas_call(
        fused_kernel,
        out_shape=jax.ShapeDtypeStruct((256, 128), f32),
        in_specs=[anywhere] * 3 + [vmem] + [anywhere] * 7,
        out_specs=vmem,
        scratch_shapes=[
            pltpu.VMEM((TILES * rows, 4096), bf16),
            pltpu.VMEM((4096, 128), bf16),
            pltpu.VMEM((4, 8192), f32),
            pltpu.VMEM((128, 512), bf16),
            pltpu.VMEM((128, 512), bf16),
            pltpu.VMEM((512, 128), bf16),
            pltpu.VMEM(first.shape, bf16),
            pltpu.VMEM(last.shape, bf16),
            pltpu.VMEM(middle.shape, bf16),
            pltpu.VMEM(twist.shape, f32),
            pltpu.VMEM((TILES, 2, 4, 4) + tile, f32),
            pltpu.VMEM((TILES, 4, 4) + tile, f32),
            pltpu.VMEM((TILES, 4, 4) + tile, f32),
            pltpu.VMEM((TILES, 4, 4) + tile, f32),
            pltpu.VMEM((TILES, 2, 4) + tile, f32),
            pltpu.VMEM((TILES, 2, 4) + tile, f32),
            pltpu.VMEM((TILES, 4) + tile, f32),
            pltpu.VMEM((TILES, 4) + tile, f32),
            pltpu.VMEM((TILES, 4) + tile, f32),
            pltpu.VMEM((32, 8, 128), f32),
            pltpu.VMEM((32, 8, 128), f32),
            pltpu.VMEM((32, 8, 128), f32),
            pltpu.VMEM((32, 8, 128), f32),
            pltpu.VMEM((2, 128, 256), f32),
            dma((TILES,)), dma((9,)),
            dma((TILES,)), dma((TILES,)), dma((TILES,)), dma((TILES,)),
            dma((TILES,)), dma((TILES,)), dma((TILES,)), dma((TILES,)),
            dma((TILES, 4)), dma((TILES, 4)), dma((32,)), dma((32,)),
        ],
        compiler_params=pltpu.CompilerParams(
            collective_id=0, has_side_effects=True, vmem_limit_bytes=56 * 1024 * 1024
        ),
    )(
        spikes, read_in, kernel, gain.reshape(1, 128), w_gate, w_up, w_down,
        jnp.asarray(first), jnp.asarray(last), jnp.asarray(middle), jnp.asarray(twist),
    ).astype(bf16)


def solution(mesh):
    placed = (P("tm", "nrn"), P("nrn", None), P(("tm", "nrn"), None), P(), P(), P(), P())
    small = mesh.shape["tm"] == 4 and mesh.shape["nrn"] == 8
    return jax.shard_map(
        fused if small else per_device,
        mesh=mesh, in_specs=placed, out_specs=P(("tm", "nrn"), None), check_vma=False,
    )
```

```python
import math

import jax
import jax.numpy as jnp
import ml_dtypes
import numpy as np
from jax import lax
from jax.experimental import pallas as pl
from jax.experimental.pallas import tpu as pltpu
from jax.sharding import PartitionSpec as P

MESH = pl.DeviceIdType.MESH
TILE_BINS = 1
TILES = 8
AHEAD = 4
LAG = 4

precise = lax.Precision.HIGHEST


def dft_table(order):
    index = jnp.arange(order, dtype=jnp.int32)
    phase = index[:, None] * index[None, :] % order
    angles = phase.astype(jnp.float32) * (2.0 * math.pi / order)
    return (jnp.cos(angles), jnp.sin(angles))


def twiddle_table(outer, inner):
    outer_index = jnp.arange(outer, dtype=jnp.int32)
    inner_index = jnp.arange(inner, dtype=jnp.int32)
    phase = outer_index[:, None] * inner_index[None, :] % (outer * inner)
    angles = phase.astype(jnp.float32) * (2.0 * math.pi / (outer * inner))
    return (jnp.cos(angles), jnp.sin(angles))


def forward_dft(signal, tables):
    cos_outer, sin_outer, cos_twist, sin_twist, cos_inner, sin_inner = tables
    real_part = jnp.einsum("ar,crs->cas", cos_outer, signal, precision=precise)
    imag_part = -jnp.einsum("ar,crs->cas", sin_outer, signal, precision=precise)
    twist_real = real_part * cos_twist + imag_part * sin_twist
    twist_imag = imag_part * cos_twist - real_part * sin_twist
    spec_real = jnp.einsum("cas,sb->cab", twist_real, cos_inner, precision=precise) + jnp.einsum(
        "cas,sb->cab", twist_imag, sin_inner, precision=precise
    )
    spec_imag = jnp.einsum("cas,sb->cab", twist_imag, cos_inner, precision=precise) - jnp.einsum(
        "cas,sb->cab", twist_real, sin_inner, precision=precise
    )
    return (spec_real, spec_imag)


def inverse_dft(spec_real, spec_imag, tables):
    cos_outer, sin_outer, cos_twist, sin_twist, cos_inner, sin_inner = tables
    back_real = jnp.einsum("cab,bs->cas", spec_real, cos_inner, precision=precise) - jnp.einsum(
        "cab,bs->cas", spec_imag, sin_inner, precision=precise
    )
    back_imag = jnp.einsum("cab,bs->cas", spec_real, sin_inner, precision=precise) + jnp.einsum(
        "cab,bs->cas", spec_imag, cos_inner, precision=precise
    )
    turn_real = back_real * cos_twist - back_imag * sin_twist
    turn_imag = back_real * sin_twist + back_imag * cos_twist
    result = jnp.einsum("ra,cas->crs", cos_outer, turn_real, precision=precise) - jnp.einsum(
        "ra,cas->crs", sin_outer, turn_imag, precision=precise
    )
    return result / (cos_outer.shape[0] * cos_inner.shape[0])


def per_device(spikes, read_in, kernel, gain, w_gate, w_up, w_down):
    time_groups = lax.axis_size("tm")
    neuron_groups = lax.axis_size("nrn")
    devices = time_groups * neuron_groups
    tok_rows = spikes.shape[0] // neuron_groups
    latent_width = read_in.shape[1]
    channels_dev = latent_width // devices
    session = tok_rows * devices
    latent = lax.psum_scatter(
        jnp.dot(spikes, read_in, preferred_element_type=jnp.float32),
        "nrn",
        scatter_dimension=0,
        tiled=True,
    )
    flipped = latent.T
    series = lax.all_to_all(flipped, ("tm", "nrn"), split_axis=0, concat_axis=1, tiled=True)
    cos_outer, sin_outer = dft_table(devices)
    cos_inner, sin_inner = dft_table(tok_rows)
    cos_twist, sin_twist = twiddle_table(devices, tok_rows)
    tables = (cos_outer, sin_outer, cos_twist, sin_twist, cos_inner, sin_inner)
    data_real, data_imag = forward_dft(series.reshape(channels_dev, devices, tok_rows), tables)
    kern_real, kern_imag = forward_dft(kernel.reshape(channels_dev, devices, tok_rows), tables)
    prod_real = data_real * kern_real - data_imag * kern_imag
    prod_imag = data_real * kern_imag + data_imag * kern_real
    conv = inverse_dft(prod_real, prod_imag, tables).reshape(channels_dev, session)
    mixed = series + conv
    stacked = lax.all_to_all(mixed, ("tm", "nrn"), split_axis=1, concat_axis=0, tiled=True)
    residual = stacked.T
    return gated_mlp(residual, gain, w_gate, w_up, w_down)


def gated_mlp(residual, gain, w_gate, w_up, w_down):
    meansq = jnp.mean(residual * residual, axis=-1, keepdims=True)
    normed = (residual * lax.rsqrt(meansq + 1e-05) * gain).astype(jnp.bfloat16)
    gate = jnp.dot(normed, w_gate, preferred_element_type=jnp.float32)
    upper = jnp.dot(normed, w_up, preferred_element_type=jnp.float32)
    act = (jax.nn.silu(gate) * upper).astype(jnp.bfloat16)
    return (residual + jnp.dot(act, w_down, preferred_element_type=jnp.float32)).astype(
        jnp.bfloat16
    )


def split(value):
    high = value.astype(jnp.bfloat16)
    low = (value - high.astype(jnp.float32)).astype(jnp.bfloat16)
    return high, low


def session_tables():
    outer, inner = 32, 256
    angle = lambda rows, columns, order: (
        2.0 * np.pi / order * (np.outer(np.arange(rows), np.arange(columns)) % order)
    )

    def parts(table):
        table = table.astype(np.float32)
        high = table.astype(ml_dtypes.bfloat16)
        low = (table - high.astype(np.float32)).astype(ml_dtypes.bfloat16)
        return high, low

    around = angle(outer, outer, outer)
    high, low = parts(np.concatenate([np.cos(around), -np.sin(around)], 0))
    first = np.concatenate([high, low, high], 1)
    high, low = parts(np.concatenate([np.cos(around), -np.sin(around)], 1))
    last = np.concatenate([high, low, high], 1)
    within = angle(inner, inner, inner)
    cosine, sine = np.cos(within), np.sin(within)
    mid_high, mid_low = parts(np.block([[cosine, -sine], [sine, cosine]]))
    turn = angle(outer, inner, outer * inner)
    twist = np.stack([np.cos(turn), np.sin(turn)]).astype(np.float32)
    return first, last, np.stack([mid_high, mid_low]), twist


def fused_kernel(
    spikes, read_in, kernel, first, last, middle, twist,
    out,
    spk_v, rd_v, ker_v, first_v, last_v, mid_v, twist_v,
    own, sib, acc, parts, xsend, xall, ysend, yall, spec, work,
    spk_sem, tab_sem, sib_s, sib_r, z_s, z_r, x_s, x_r, y_s, y_r,
):
    tm, nrn = lax.axis_index("tm"), lax.axis_index("nrn")
    me = tm * 8 + nrn
    z, core = lax.div(nrn, 2), lax.rem(nrn, 2)
    rows = TILE_BINS * 256

    def spike_copy(k):
        where = pl.ds(pl.multiple_of(k * rows, rows), rows)
        return pltpu.make_async_copy(spikes.at[where], spk_v.at[k], spk_sem.at[k])

    loads = [
        pltpu.make_async_copy(source, target, tab_sem.at[i])
        for i, (source, target) in enumerate(
            [
                (read_in, rd_v), (kernel, ker_v), (first, first_v), (twist, twist_v),
                (middle, mid_v), (last, last_v),
            ]
        )
    ]
    loads[0].start()
    for k in range(AHEAD):
        spike_copy(k).start()

    barrier = pltpu.get_barrier_semaphore()

    def after(d):
        other = lax.rem(me + d, 32)
        return (lax.div(other, 8), lax.rem(other, 8))

    def greet(d, carry):
        pl.semaphore_signal(barrier, inc=1, device_id=after(d), device_id_type=MESH)
        return carry

    lax.fori_loop(1, 32, greet, 0)
    loads[0].wait()

    def remote(source, target, send, recv, where):
        return pltpu.make_async_remote_copy(
            src_ref=source, dst_ref=target, send_sem=send, recv_sem=recv,
            device_id=where, device_id_type=MESH,
        )

    def sib_copy(k):
        return remote(own.at[k, 1 - core], sib.at[k], sib_s.at[k], sib_r.at[k], (tm, z * 2 + 1 - core))

    def z_copy(k, d):
        other = lax.rem(z + d, 4)
        return remote(acc.at[k, other], parts.at[k, d - 1], z_s.at[k, d], z_r.at[k, d], (tm, other * 2 + core))

    def x_copy(k, d):
        other = lax.rem(tm + d, 4)
        return remote(
            xsend.at[k, other], xall.at[1, pl.ds(tm * 8 + k * TILE_BINS, TILE_BINS)],
            x_s.at[k, d], x_r.at[k, d], (other, nrn),
        )

    def tile_step(k, carry):
        @pl.when(k < TILES)
        def _():
            @pl.when(k + AHEAD < TILES)
            def _():
                spike_copy(k + AHEAD).start()

            @pl.when(k == AHEAD)
            def _():
                for load in loads[1:]:
                    load.start()

            spike_copy(k).wait()
            sums = jnp.dot(spk_v[k], rd_v[...], preferred_element_type=jnp.float32)
            for b in range(TILE_BINS):
                low = sums[b * 256 : b * 256 + 128].T
                high = sums[b * 256 + 128 : b * 256 + 256].T
                for g in range(32):
                    piece = jnp.concatenate([low[4 * g : 4 * g + 4], high[4 * g : 4 * g + 4]], 0)
                    own[k, g % 2, (g % 8) // 2, g // 8, b] = piece

            @pl.when(k == 0)
            def _():
                pl.semaphore_wait(barrier, 31)

            sib_copy(k).start()

        @pl.when(k >= 1)
        def _():
            sib_copy(k - 1).wait_recv()
            acc[k - 1] = own[k - 1, core] + sib[k - 1]
            for d in (2, 1, 3):
                z_copy(k - 1, d).start()

        @pl.when((k >= LAG) & (k < TILES))
        def _():
            finish_sum(k - LAG)

        return carry

    def finish_sum(k):
        for d in (1, 2, 3):
            z_copy(k, d).wait_recv()
        xsend[k] = acc[k, z] + parts[k, 0] + parts[k, 1] + parts[k, 2]
        for d in (3, 1, 2):
            x_copy(k, d).start()
        xall[1, pl.ds(tm * 8 + k * TILE_BINS, TILE_BINS)] = xsend[k, tm]

    lax.fori_loop(0, TILES + 1, tile_step, 0)

    for load in loads[1:]:
        load.wait()
    for r in range(32):
        for half in range(2):
            xall[0, r, half * 4 : half * 4 + 4, :] = ker_v[:, r * 256 + half * 128 : r * 256 + half * 128 + 128]

    cos_turn = jnp.concatenate([twist_v[0]] * 4, 1)
    sin_turn = jnp.concatenate([twist_v[1]] * 4, 1)

    def stacked(value):
        high, low = split(value)
        return jnp.concatenate([high, high, low], 0)

    def to_rows(value):
        return jnp.concatenate([value[:, 256 * j : 256 * j + 256] for j in range(4)], 0)

    def to_lanes(value):
        return jnp.concatenate([value[32 * j : 32 * j + 32] for j in range(4)], 1)

    def inner_dft(real, imag):
        high, low = split(jnp.concatenate([real, imag], 1))
        both = jnp.concatenate([high, low], 0)
        result = jnp.dot(both, mid_v[0], preferred_element_type=jnp.float32)
        result = result[:128] + result[128:]
        result += jnp.dot(high, mid_v[1], preferred_element_type=jnp.float32)
        return result[:, :256], result[:, 256:]

    def gather_lanes(p):
        return jnp.concatenate([xall[p, :, half * 4 + j, :] for j in range(4) for half in range(2)], 1)

    def outer_dft(signal):
        both = jnp.dot(first_v[...], stacked(signal), preferred_element_type=jnp.float32)
        real, imag = both[:32], both[32:]
        turned_real = real * cos_turn + imag * sin_turn
        turned_imag = imag * cos_turn - real * sin_turn
        return to_rows(turned_real), to_rows(turned_imag)

    def dft_pass(p, carry):
        @pl.when(p < 2)
        def _():
            work[0], work[1] = outer_dft(gather_lanes(p))

        real, imag = inner_dft(work[0], work[1])

        @pl.when(p == 0)
        def _():
            spec[0] = real * (1.0 / 8192)
            spec[1] = imag * (1.0 / 8192)

            def late_finish(k, carry):
                finish_sum(k)
                return carry

            lax.fori_loop(TILES - LAG, TILES, late_finish, 0)

            def x_arrived(k, carry):
                for d in (1, 2, 3):
                    x_copy(k, d).wait_recv()
                return carry

            lax.fori_loop(0, TILES, x_arrived, 0)

        @pl.when(p == 1)
        def _():
            work[0] = real * spec[0] - imag * spec[1]
            work[1] = -(real * spec[1] + imag * spec[0])

        @pl.when(p == 2)
        def _():
            work[0] = real
            work[1] = imag

        return carry

    lax.fori_loop(0, 3, dft_pass, 0)
    series = gather_lanes(1)
    back_real, back_neg = to_lanes(work[0]), to_lanes(work[1])
    turned = jnp.concatenate(
        [back_real * cos_turn + back_neg * sin_turn, back_real * sin_turn - back_neg * cos_turn], 0
    )
    mixed = series + jnp.dot(last_v[...], stacked(turned), preferred_element_type=jnp.float32)
    for m in range(8):
        ysend[:, m, :] = mixed[:, 128 * m : 128 * m + 128]

    def y_copy(d):
        other = lax.rem(me + d, 32)
        return remote(ysend.at[other], yall.at[me], y_s.at[d], y_r.at[d], after(d))

    def y_start(d, carry):
        y_copy(d).start()
        return carry

    lax.fori_loop(1, 32, y_start, 0)
    yall[me] = ysend[me]

    def drain(k, carry):
        sib_copy(k).wait_send()
        for d in (1, 2, 3):
            z_copy(k, d).wait_send()
            x_copy(k, d).wait_send()
        return carry

    lax.fori_loop(0, TILES, drain, 0)

    def y_wait(d, carry):
        y_copy(d).wait()
        return carry

    lax.fori_loop(1, 32, y_wait, 0)

    flat = yall.reshape(256, 128)
    for half in range(2):
        out[half * 128 : half * 128 + 128, :] = flat[pl.ds(half, 128, stride=2), :].T


def fused(spikes, read_in, kernel, gain, w_gate, w_up, w_down):
    first, last, middle, twist = session_tables()
    f32, bf16 = jnp.float32, jnp.bfloat16
    tile = (TILE_BINS, 8, 128)
    rows = TILE_BINS * 256
    dma = pltpu.SemaphoreType.DMA
    anywhere = pl.BlockSpec(memory_space=pl.ANY)
    vmem = pl.BlockSpec(memory_space=pltpu.VMEM)
    residual = pl.pallas_call(
        fused_kernel,
        out_shape=jax.ShapeDtypeStruct((256, 128), f32),
        in_specs=[anywhere] * 7,
        out_specs=vmem,
        scratch_shapes=[
            pltpu.VMEM((TILES, rows, 4096), bf16),
            pltpu.VMEM((4096, 128), bf16),
            pltpu.VMEM((4, 8192), f32),
            pltpu.VMEM(first.shape, bf16),
            pltpu.VMEM(last.shape, bf16),
            pltpu.VMEM(middle.shape, bf16),
            pltpu.VMEM(twist.shape, f32),
            pltpu.VMEM((TILES, 2, 4, 4) + tile, f32),
            pltpu.VMEM((TILES, 4, 4) + tile, f32),
            pltpu.VMEM((TILES, 4, 4) + tile, f32),
            pltpu.VMEM((TILES, 3, 4) + tile, f32),
            pltpu.VMEM((TILES, 4) + tile, f32),
            pltpu.VMEM((2, 32, 8, 128), f32),
            pltpu.VMEM((32, 8, 128), f32),
            pltpu.VMEM((32, 8, 128), f32),
            pltpu.VMEM((2, 128, 256), f32),
            pltpu.VMEM((2, 128, 256), f32),
            dma((TILES,)), dma((6,)), dma((TILES,)), dma((TILES,)),
            dma((TILES, 4)), dma((TILES, 4)), dma((TILES, 4)), dma((TILES, 4)), dma((32,)), dma((32,)),
        ],
        compiler_params=pltpu.CompilerParams(
            collective_id=0, has_side_effects=True, vmem_limit_bytes=56 * 1024 * 1024
        ),
    )(
        spikes, read_in, kernel,
        jnp.asarray(first), jnp.asarray(last), jnp.asarray(middle), jnp.asarray(twist),
    )
    return gated_mlp(residual, gain, w_gate, w_up, w_down)


def solution(mesh):
    placed = (P("tm", "nrn"), P("nrn", None), P(("tm", "nrn"), None), P(), P(), P(), P())
    small = mesh.shape["tm"] == 4 and mesh.shape["nrn"] == 8
    return jax.shard_map(
        fused if small else per_device,
        mesh=mesh, in_specs=placed, out_specs=P(("tm", "nrn"), None), check_vma=False,
    )
```

```python
import math

import jax
import jax.numpy as jnp
import ml_dtypes
import numpy as np
from jax import lax
from jax.experimental import pallas as pl
from jax.experimental.pallas import tpu as pltpu
from jax.sharding import PartitionSpec as P

MESH = pl.DeviceIdType.MESH
TILE_BINS = 1
TILES = 8
AHEAD = 4
LAG = 4

precise = lax.Precision.HIGHEST


def dft_table(order):
    index = jnp.arange(order, dtype=jnp.int32)
    phase = index[:, None] * index[None, :] % order
    angles = phase.astype(jnp.float32) * (2.0 * math.pi / order)
    return (jnp.cos(angles), jnp.sin(angles))


def twiddle_table(outer, inner):
    outer_index = jnp.arange(outer, dtype=jnp.int32)
    inner_index = jnp.arange(inner, dtype=jnp.int32)
    phase = outer_index[:, None] * inner_index[None, :] % (outer * inner)
    angles = phase.astype(jnp.float32) * (2.0 * math.pi / (outer * inner))
    return (jnp.cos(angles), jnp.sin(angles))


def forward_dft(signal, tables):
    cos_outer, sin_outer, cos_twist, sin_twist, cos_inner, sin_inner = tables
    real_part = jnp.einsum("ar,crs->cas", cos_outer, signal, precision=precise)
    imag_part = -jnp.einsum("ar,crs->cas", sin_outer, signal, precision=precise)
    twist_real = real_part * cos_twist + imag_part * sin_twist
    twist_imag = imag_part * cos_twist - real_part * sin_twist
    spec_real = jnp.einsum("cas,sb->cab", twist_real, cos_inner, precision=precise) + jnp.einsum(
        "cas,sb->cab", twist_imag, sin_inner, precision=precise
    )
    spec_imag = jnp.einsum("cas,sb->cab", twist_imag, cos_inner, precision=precise) - jnp.einsum(
        "cas,sb->cab", twist_real, sin_inner, precision=precise
    )
    return (spec_real, spec_imag)


def inverse_dft(spec_real, spec_imag, tables):
    cos_outer, sin_outer, cos_twist, sin_twist, cos_inner, sin_inner = tables
    back_real = jnp.einsum("cab,bs->cas", spec_real, cos_inner, precision=precise) - jnp.einsum(
        "cab,bs->cas", spec_imag, sin_inner, precision=precise
    )
    back_imag = jnp.einsum("cab,bs->cas", spec_real, sin_inner, precision=precise) + jnp.einsum(
        "cab,bs->cas", spec_imag, cos_inner, precision=precise
    )
    turn_real = back_real * cos_twist - back_imag * sin_twist
    turn_imag = back_real * sin_twist + back_imag * cos_twist
    result = jnp.einsum("ra,cas->crs", cos_outer, turn_real, precision=precise) - jnp.einsum(
        "ra,cas->crs", sin_outer, turn_imag, precision=precise
    )
    return result / (cos_outer.shape[0] * cos_inner.shape[0])


def per_device(spikes, read_in, kernel, gain, w_gate, w_up, w_down):
    time_groups = lax.axis_size("tm")
    neuron_groups = lax.axis_size("nrn")
    devices = time_groups * neuron_groups
    tok_rows = spikes.shape[0] // neuron_groups
    latent_width = read_in.shape[1]
    channels_dev = latent_width // devices
    session = tok_rows * devices
    latent = lax.psum_scatter(
        jnp.dot(spikes, read_in, preferred_element_type=jnp.float32),
        "nrn",
        scatter_dimension=0,
        tiled=True,
    )
    flipped = latent.T
    series = lax.all_to_all(flipped, ("tm", "nrn"), split_axis=0, concat_axis=1, tiled=True)
    cos_outer, sin_outer = dft_table(devices)
    cos_inner, sin_inner = dft_table(tok_rows)
    cos_twist, sin_twist = twiddle_table(devices, tok_rows)
    tables = (cos_outer, sin_outer, cos_twist, sin_twist, cos_inner, sin_inner)
    data_real, data_imag = forward_dft(series.reshape(channels_dev, devices, tok_rows), tables)
    kern_real, kern_imag = forward_dft(kernel.reshape(channels_dev, devices, tok_rows), tables)
    prod_real = data_real * kern_real - data_imag * kern_imag
    prod_imag = data_real * kern_imag + data_imag * kern_real
    conv = inverse_dft(prod_real, prod_imag, tables).reshape(channels_dev, session)
    mixed = series + conv
    stacked = lax.all_to_all(mixed, ("tm", "nrn"), split_axis=1, concat_axis=0, tiled=True)
    residual = stacked.T
    return gated_mlp(residual, gain, w_gate, w_up, w_down)


def gated_mlp(residual, gain, w_gate, w_up, w_down):
    meansq = jnp.mean(residual * residual, axis=-1, keepdims=True)
    normed = (residual * lax.rsqrt(meansq + 1e-05) * gain).astype(jnp.bfloat16)
    gate = jnp.dot(normed, w_gate, preferred_element_type=jnp.float32)
    upper = jnp.dot(normed, w_up, preferred_element_type=jnp.float32)
    act = (jax.nn.silu(gate) * upper).astype(jnp.bfloat16)
    return (residual + jnp.dot(act, w_down, preferred_element_type=jnp.float32)).astype(
        jnp.bfloat16
    )


def split(value):
    high = value.astype(jnp.bfloat16)
    low = (value - high.astype(jnp.float32)).astype(jnp.bfloat16)
    return high, low


def session_tables():
    outer, inner = 32, 256
    angle = lambda rows, columns, order: (
        2.0 * np.pi / order * (np.outer(np.arange(rows), np.arange(columns)) % order)
    )

    def parts(table):
        table = table.astype(np.float32)
        high = table.astype(ml_dtypes.bfloat16)
        low = (table - high.astype(np.float32)).astype(ml_dtypes.bfloat16)
        return high, low

    around = angle(outer, outer, outer)
    high, low = parts(np.concatenate([np.cos(around), -np.sin(around)], 0))
    first = np.concatenate([high, low, high], 1)
    high, low = parts(np.concatenate([np.cos(around), -np.sin(around)], 1))
    last = np.concatenate([high, low, high], 1)
    within = angle(inner, inner, inner)
    cosine, sine = np.cos(within), np.sin(within)
    mid_high, mid_low = parts(np.block([[cosine, -sine], [sine, cosine]]))
    turn = angle(outer, inner, outer * inner)
    twist = np.stack([np.cos(turn), np.sin(turn)]).astype(np.float32)
    return first, last, np.stack([mid_high, mid_low]), twist


def fused_kernel(
    spikes, read_in, kernel, gain, w_gate, w_up, w_down, first, last, middle, twist,
    out,
    spk_v, rd_v, ker_v, wg_v, wu_v, wd_v, first_v, last_v, mid_v, twist_v,
    own, sib, acc, parts, xsend, xall, ysend, yall, spec, work,
    spk_sem, tab_sem, sib_s, sib_r, z_s, z_r, x_s, x_r, y_s, y_r,
):
    tm, nrn = lax.axis_index("tm"), lax.axis_index("nrn")
    me = tm * 8 + nrn
    z, core = lax.div(nrn, 2), lax.rem(nrn, 2)
    rows = TILE_BINS * 256

    def spike_copy(k):
        where = pl.ds(pl.multiple_of(k * rows, rows), rows)
        return pltpu.make_async_copy(spikes.at[where], spk_v.at[k], spk_sem.at[k])

    loads = [
        pltpu.make_async_copy(source, target, tab_sem.at[i])
        for i, (source, target) in enumerate(
            [
                (read_in, rd_v), (kernel, ker_v), (first, first_v), (twist, twist_v),
                (middle, mid_v), (last, last_v), (w_gate, wg_v), (w_up, wu_v), (w_down, wd_v),
            ]
        )
    ]
    loads[0].start()
    for k in range(AHEAD):
        spike_copy(k).start()

    barrier = pltpu.get_barrier_semaphore()

    def after(d):
        other = lax.rem(me + d, 32)
        return (lax.div(other, 8), lax.rem(other, 8))

    def greet(d, carry):
        pl.semaphore_signal(barrier, inc=1, device_id=after(d), device_id_type=MESH)
        return carry

    lax.fori_loop(1, 32, greet, 0)
    loads[0].wait()

    def remote(source, target, send, recv, where):
        return pltpu.make_async_remote_copy(
            src_ref=source, dst_ref=target, send_sem=send, recv_sem=recv,
            device_id=where, device_id_type=MESH,
        )

    def sib_copy(k):
        return remote(own.at[k, 1 - core], sib.at[k], sib_s.at[k], sib_r.at[k], (tm, z * 2 + 1 - core))

    def z_copy(k, d):
        other = lax.rem(z + d, 4)
        return remote(acc.at[k, other], parts.at[k, d - 1], z_s.at[k, d], z_r.at[k, d], (tm, other * 2 + core))

    def x_copy(k, d):
        other = lax.rem(tm + d, 4)
        return remote(
            xsend.at[k, other], xall.at[1, pl.ds(tm * 8 + k * TILE_BINS, TILE_BINS)],
            x_s.at[k, d], x_r.at[k, d], (other, nrn),
        )

    def tile_step(k, carry):
        @pl.when(k < TILES)
        def _():
            @pl.when(k + AHEAD < TILES)
            def _():
                spike_copy(k + AHEAD).start()

            @pl.when(k == AHEAD)
            def _():
                for load in loads[1:]:
                    load.start()

            spike_copy(k).wait()
            sums = jnp.dot(spk_v[k], rd_v[...], preferred_element_type=jnp.float32)
            for b in range(TILE_BINS):
                low = sums[b * 256 : b * 256 + 128].T
                high = sums[b * 256 + 128 : b * 256 + 256].T
                for g in range(32):
                    piece = jnp.concatenate([low[4 * g : 4 * g + 4], high[4 * g : 4 * g + 4]], 0)
                    own[k, g % 2, (g % 8) // 2, g // 8, b] = piece

            @pl.when(k == 0)
            def _():
                pl.semaphore_wait(barrier, 31)

            sib_copy(k).start()

        @pl.when(k >= 1)
        def _():
            sib_copy(k - 1).wait_recv()
            acc[k - 1] = own[k - 1, core] + sib[k - 1]
            for d in (2, 1, 3):
                z_copy(k - 1, d).start()

        @pl.when((k >= LAG) & (k < TILES))
        def _():
            finish_sum(k - LAG)

        return carry

    def finish_sum(k):
        for d in (1, 2, 3):
            z_copy(k, d).wait_recv()
        xsend[k] = acc[k, z] + parts[k, 0] + parts[k, 1] + parts[k, 2]
        for d in (3, 1, 2):
            x_copy(k, d).start()
        xall[1, pl.ds(tm * 8 + k * TILE_BINS, TILE_BINS)] = xsend[k, tm]

    lax.fori_loop(0, TILES + 1, tile_step, 0)

    for load in loads[1:]:
        load.wait()
    for r in range(32):
        for half in range(2):
            xall[0, r, half * 4 : half * 4 + 4, :] = ker_v[:, r * 256 + half * 128 : r * 256 + half * 128 + 128]

    cos_turn = jnp.concatenate([twist_v[0]] * 4, 1)
    sin_turn = jnp.concatenate([twist_v[1]] * 4, 1)

    def stacked(value):
        high, low = split(value)
        return jnp.concatenate([high, high, low], 0)

    def to_rows(value):
        return jnp.concatenate([value[:, 256 * j : 256 * j + 256] for j in range(4)], 0)

    def to_lanes(value):
        return jnp.concatenate([value[32 * j : 32 * j + 32] for j in range(4)], 1)

    def inner_dft(real, imag):
        high, low = split(jnp.concatenate([real, imag], 1))
        both = jnp.concatenate([high, low], 0)
        result = jnp.dot(both, mid_v[0], preferred_element_type=jnp.float32)
        result = result[:128] + result[128:]
        result += jnp.dot(high, mid_v[1], preferred_element_type=jnp.float32)
        return result[:, :256], result[:, 256:]

    def gather_lanes(p):
        return jnp.concatenate([xall[p, :, half * 4 + j, :] for j in range(4) for half in range(2)], 1)

    def outer_dft(signal):
        both = jnp.dot(first_v[...], stacked(signal), preferred_element_type=jnp.float32)
        real, imag = both[:32], both[32:]
        turned_real = real * cos_turn + imag * sin_turn
        turned_imag = imag * cos_turn - real * sin_turn
        return to_rows(turned_real), to_rows(turned_imag)

    def dft_pass(p, carry):
        @pl.when(p < 2)
        def _():
            work[0], work[1] = outer_dft(gather_lanes(p))

        real, imag = inner_dft(work[0], work[1])

        @pl.when(p == 0)
        def _():
            spec[0] = real * (1.0 / 8192)
            spec[1] = imag * (1.0 / 8192)

            def late_finish(k, carry):
                finish_sum(k)
                return carry

            lax.fori_loop(TILES - LAG, TILES, late_finish, 0)

            def x_arrived(k, carry):
                for d in (1, 2, 3):
                    x_copy(k, d).wait_recv()
                return carry

            lax.fori_loop(0, TILES, x_arrived, 0)

        @pl.when(p == 1)
        def _():
            work[0] = real * spec[0] - imag * spec[1]
            work[1] = -(real * spec[1] + imag * spec[0])

        @pl.when(p == 2)
        def _():
            work[0] = real
            work[1] = imag

        return carry

    lax.fori_loop(0, 3, dft_pass, 0)
    series = gather_lanes(1)
    back_real, back_neg = to_lanes(work[0]), to_lanes(work[1])
    turned = jnp.concatenate(
        [back_real * cos_turn + back_neg * sin_turn, back_real * sin_turn - back_neg * cos_turn], 0
    )
    mixed = series + jnp.dot(last_v[...], stacked(turned), preferred_element_type=jnp.float32)
    for m in range(8):
        ysend[:, m, :] = mixed[:, 128 * m : 128 * m + 128]

    def y_copy(d):
        other = lax.rem(me + d, 32)
        return remote(ysend.at[other], yall.at[me], y_s.at[d], y_r.at[d], after(d))

    def y_start(d, carry):
        y_copy(d).start()
        return carry

    lax.fori_loop(1, 32, y_start, 0)
    yall[me] = ysend[me]

    def drain(k, carry):
        sib_copy(k).wait_send()
        for d in (1, 2, 3):
            z_copy(k, d).wait_send()
            x_copy(k, d).wait_send()
        return carry

    lax.fori_loop(0, TILES, drain, 0)

    def y_wait(d, carry):
        y_copy(d).wait()
        return carry

    lax.fori_loop(1, 32, y_wait, 0)

    flat = yall.reshape(256, 128)
    residual = jnp.concatenate([flat[pl.ds(half, 128, stride=2), :].T for half in range(2)], 0)
    meansq = jnp.mean(residual * residual, axis=-1, keepdims=True)
    normed = (residual * lax.rsqrt(meansq + 1e-05) * gain[...]).astype(jnp.bfloat16)
    gate = jnp.dot(normed, wg_v[...], preferred_element_type=jnp.float32)
    upper = jnp.dot(normed, wu_v[...], preferred_element_type=jnp.float32)
    act = (gate / (1.0 + jnp.exp(-gate)) * upper).astype(jnp.bfloat16)
    out[...] = (residual + jnp.dot(act, wd_v[...], preferred_element_type=jnp.float32)).astype(jnp.bfloat16)


def fused(spikes, read_in, kernel, gain, w_gate, w_up, w_down):
    first, last, middle, twist = session_tables()
    f32, bf16 = jnp.float32, jnp.bfloat16
    tile = (TILE_BINS, 8, 128)
    rows = TILE_BINS * 256
    dma = pltpu.SemaphoreType.DMA
    anywhere = pl.BlockSpec(memory_space=pl.ANY)
    vmem = pl.BlockSpec(memory_space=pltpu.VMEM)
    return pl.pallas_call(
        fused_kernel,
        out_shape=jax.ShapeDtypeStruct((256, 128), bf16),
        in_specs=[anywhere] * 3 + [vmem] + [anywhere] * 7,
        out_specs=vmem,
        scratch_shapes=[
            pltpu.VMEM((TILES, rows, 4096), bf16),
            pltpu.VMEM((4096, 128), bf16),
            pltpu.VMEM((4, 8192), f32),
            pltpu.VMEM((128, 512), bf16),
            pltpu.VMEM((128, 512), bf16),
            pltpu.VMEM((512, 128), bf16),
            pltpu.VMEM(first.shape, bf16),
            pltpu.VMEM(last.shape, bf16),
            pltpu.VMEM(middle.shape, bf16),
            pltpu.VMEM(twist.shape, f32),
            pltpu.VMEM((TILES, 2, 4, 4) + tile, f32),
            pltpu.VMEM((TILES, 4, 4) + tile, f32),
            pltpu.VMEM((TILES, 4, 4) + tile, f32),
            pltpu.VMEM((TILES, 3, 4) + tile, f32),
            pltpu.VMEM((TILES, 4) + tile, f32),
            pltpu.VMEM((2, 32, 8, 128), f32),
            pltpu.VMEM((32, 8, 128), f32),
            pltpu.VMEM((32, 8, 128), f32),
            pltpu.VMEM((2, 128, 256), f32),
            pltpu.VMEM((2, 128, 256), f32),
            dma((TILES,)), dma((9,)), dma((TILES,)), dma((TILES,)),
            dma((TILES, 4)), dma((TILES, 4)), dma((TILES, 4)), dma((TILES, 4)), dma((32,)), dma((32,)),
        ],
        compiler_params=pltpu.CompilerParams(
            collective_id=0, has_side_effects=True, vmem_limit_bytes=56 * 1024 * 1024
        ),
    )(
        spikes, read_in, kernel, gain.reshape(1, 128), w_gate, w_up, w_down,
        jnp.asarray(first), jnp.asarray(last), jnp.asarray(middle), jnp.asarray(twist),
    )


def solution(mesh):
    placed = (P("tm", "nrn"), P("nrn", None), P(("tm", "nrn"), None), P(), P(), P(), P())
    small = mesh.shape["tm"] == 4 and mesh.shape["nrn"] == 8
    return jax.shard_map(
        fused if small else per_device,
        mesh=mesh, in_specs=placed, out_specs=P(("tm", "nrn"), None), check_vma=False,
    )
```
